32 devices in a mesh: parts: 2 (over x), row: 16 (over z, y, core).
Axes of the slice: x: 2, y: 2, z: 4, core: 2. Of those that a mesh axis runs over, the one named last changes fastest.
Arguments:
- coords: int32 [4, 3, 512], P('parts'), parts along dimension 0, may hold values from 0 to 7
- labels: int32 [16, 16, 512], P('parts', 'row'), parts along dimension 0, may hold values from 0 to 255
- ranks: int32 [16, 16, 2], P('parts', 'row'), parts along dimension 0, may hold values from 16 to 128, as said below
- u_first: bfloat16 [16, 16, 512, 128], P('parts', 'row'), parts along dimension 0, may hold values from -6 to 6
- v_first: bfloat16 [16, 16, 512, 128], P('parts', 'row'), parts along dimension 0, may hold values from -0.0046875 to 0.0046875
- u_second: bfloat16 [16, 16, 512, 128], P('parts', 'row'), parts along dimension 0, may hold values from -6 to 6
- v_second: bfloat16 [16, 16, 512, 128], P('parts', 'row'), parts along dimension 0, may hold values from -0.01171875 to 0.01171875
Outputs:
- eliminated: float32 [16, 16, 512, 256], P('parts', 'row'), parts along dimension 0
- diagonal_factors: float32 [4, 512, 512], P('parts'), parts along dimension 0
The draws below stay inside these ranges and needn't reach their ends.
There are 2 independent parts, one for each index of `parts`. The reference program is written for one: setup_inputs(seed, part) draws one part's arguments, and reference() takes and returns one part's arrays. A program takes and returns all parts, laid end to end along the dimension named above; each array names one. Nothing has to cross between parts.
Inputs may be any that keep to these rules, and one draw needn't show every extreme that they name: `ranks`: the block of tile 1 in column 0 has rank 128; some block has rank 128 // 8.
All inputs are finite; a program needn't handle non-finite values.
Results may differ from the reference program's by a relative error of at most 0.0003.
Values may be sent and summed in bfloat16 or wider, within the bound.
A program may use at most 128 MiB of HBM per device.

```python
import math
import jax
import jax.numpy as jnp
from jax import lax

B = 512
RMAX = 128
NRHS = 256
CYCLES = 8
TILES = 128
N_ROW = 16


def draw_ranks(key, part):
    lowest = RMAX // 8
    number = 2 * TILES
    values = jax.random.randint(jax.random.fold_in(key, 11), (number,), lowest, RMAX + 1)
    second_spot = (3 + jax.random.randint(jax.random.fold_in(key, 13), (), 0, number - 1)) % number
    values = values.at[2].set(RMAX).at[second_spot].set(lowest)
    return values.reshape(CYCLES, TILES // CYCLES, 2).astype(jnp.int32)


def factor_entries(key, salt):
    shape = (CYCLES, TILES // CYCLES, B, RMAX)
    values = jnp.clip(jax.random.normal(jax.random.fold_in(key, salt), shape, jnp.float32), -6.0, 6.0)
    return values


def draw_u_first(key, part):
    return factor_entries(key, 21).astype(jnp.bfloat16)


def draw_v_first(key, part):
    return (factor_entries(key, 22) * (0.4 / B)).astype(jnp.bfloat16)


def set_ends(drawn, key, least, largest):
    spot = [jax.random.randint(jax.random.fold_in(key, axis), (), 0, length) for axis, length in enumerate(drawn.shape)]
    longest = drawn.shape.index(max(drawn.shape))
    neighbour = spot[:longest] + [(spot[longest] + 1) % drawn.shape[longest]] + spot[longest + 1:]
    return drawn.at[tuple(spot)].set(least).at[tuple(neighbour)].set(largest)


def level_of(own_key, shape, cuts, least, largest):
    factor_of, own = 1.0, jax.random.fold_in(own_key, 6)
    for axis_at, shards_of in cuts:
        steps = jnp.exp(jax.random.uniform(jax.random.fold_in(own, axis_at), (shards_of,), jnp.float32, least / len(cuts), largest / len(cuts)))
        factor_of = factor_of * jnp.repeat(steps, shape[axis_at] // shards_of).reshape([-1 if axis == axis_at else 1 for axis in range(len(shape))])
    return factor_of


def bell_draw(rng, extent, width, bound, cuts=(), kind=jnp.bfloat16):
    factor_of = level_of(rng, extent, cuts, -0.22, 0.18) if cuts else 1.0
    result = jax.random.normal(rng, extent, jnp.float32) * width * factor_of
    return jnp.minimum(jnp.maximum(result, -bound), bound).astype(kind)


def setup_inputs(seed: int = 0, part: int = 0) -> dict:
    key_of = jax.random.split(jax.random.key(seed), 8)
    part_keys = jax.random.split(jax.random.fold_in(key_of[7], part), 8)
    coords = set_ends(jax.random.randint(part_keys[0], (2, 3, B), 0, 8), jax.random.fold_in(part_keys[0], 1), 0, 7).astype(jnp.int32)
    labels = set_ends(jax.random.randint(part_keys[1], (CYCLES, N_ROW, B), 0, NRHS), jax.random.fold_in(part_keys[1], 1), 0, NRHS - 1).astype(jnp.int32)
    ranks = draw_ranks(jax.random.fold_in(jax.random.fold_in(key_of[7], part), 71), part)
    u_first = draw_u_first(jax.random.fold_in(jax.random.fold_in(key_of[7], part), 71), part)
    v_first = draw_v_first(jax.random.fold_in(jax.random.fold_in(key_of[7], part), 71), part)
    u_second = bell_draw(part_keys[5], (CYCLES, N_ROW, B, RMAX), 1.0, 6.0, ((1, 16),))
    v_second = bell_draw(part_keys[6], (CYCLES, N_ROW, B, RMAX), (0.4 / B), 0.01171875, ((1, 16),))
    return dict(coords=coords, labels=labels, ranks=ranks, u_first=u_first, v_first=v_first, u_second=u_second, v_second=v_second)


highest = lax.Precision.HIGHEST
four_pi = 4.0 * math.pi

def matmul(left, right):
    return jnp.dot(left.astype(jnp.float32), right.astype(jnp.float32), precision=highest, preferred_element_type=jnp.float32)

def kernel_tile(points):
    spots = points.astype(jnp.float32)
    distance = jnp.zeros((spots.shape[1], spots.shape[1]), jnp.float32)
    for dimension in range(3):
        offset = spots[dimension][:, None] - spots[dimension][None, :]
        distance = distance + offset * offset
    return 1.0 / (four_pi * jnp.sqrt(distance + 1.0)) + jnp.eye(spots.shape[1], dtype=jnp.float32)

def onehot(label_row):
    return (label_row[..., None] == jnp.arange(NRHS, dtype=jnp.int32)).astype(jnp.float32)

def triangular(lower, target):
    return lax.linalg.triangular_solve(lower, target, left_side=True, lower=True)

def solve_stack(lower, stack):
    number, height, breadth = stack.shape
    flat = jnp.transpose(stack, (1, 0, 2)).reshape(height, number * breadth)
    solved = triangular(lower, flat)
    return jnp.transpose(solved.reshape(height, number, breadth), (1, 0, 2))

def rank_mask(rank_values, breadth):
    columns = jnp.arange(breadth, dtype=jnp.int32)
    return (columns[None, :] < rank_values[:, None]).astype(jnp.float32)

def second_panel(points, label_row, u_one, w_one, first_sol):
    inner_gram = matmul(w_one.T, w_one)
    diagonal_tile = kernel_tile(points) - matmul(matmul(u_one, inner_gram), u_one.T)
    lower = jnp.linalg.cholesky(diagonal_tile)
    target = onehot(label_row) - matmul(u_one, matmul(w_one.T, first_sol))
    return (lower, triangular(lower, target))

def update(w_tiles, first_sol, second_lower, second_sol, u_one, w_one, label_rows, rank_rows, u0, u1, v1):
    breadth = u0.shape[-1]
    u_zero = u0.astype(jnp.float32)
    u_next = u1.astype(jnp.float32)
    v_next = v1.astype(jnp.float32) * rank_mask(rank_rows[:, 1], breadth)[:, None, :]
    first_weights = jnp.einsum('nbr,bc->nrc', w_tiles, first_sol, precision=highest)
    first_update = jnp.einsum('nbr,nrc->nbc', u_zero, first_weights, precision=highest)
    cross = jnp.einsum('br,nbs->nrs', w_one, w_tiles, precision=highest)
    mixed = -jnp.einsum('br,nrs->nbs', u_one, cross, precision=highest)
    factor = solve_stack(second_lower, jnp.concatenate([v_next, mixed], axis=-1))
    second_weights = jnp.einsum('nbk,bc->nkc', factor, second_sol, precision=highest)
    left_pair = jnp.concatenate([u_next, u_zero], axis=-1)
    second_update = jnp.einsum('nbk,nkc->nbc', left_pair, second_weights, precision=highest)
    return onehot(label_rows) - first_update - second_update

def reference(coords, labels, ranks, u_first, v_first, u_second, v_second):
    first_lower = jnp.linalg.cholesky(kernel_tile(coords[0]))
    first_sol = triangular(first_lower, onehot(labels[0, 0]))
    mask_one = rank_mask(ranks[0, 1, 0:1], RMAX)
    w_one = triangular(first_lower, v_first[0, 1].astype(jnp.float32) * mask_one)
    u_one = u_first[0, 1].astype(jnp.float32)
    second_lower, second_sol = second_panel(coords[1], labels[0, 1], u_one, w_one, first_sol)

    def per_cycle(pieces):
        label_rows, rank_rows, u0, v0, u1, v1 = pieces
        v_zero = v0.astype(jnp.float32) * rank_mask(rank_rows[:, 0], RMAX)[:, None, :]
        w_tiles = solve_stack(first_lower, v_zero)
        return update(w_tiles, first_sol, second_lower, second_sol, u_one, w_one, label_rows, rank_rows, u0, u1, v1)
    updated = lax.map(per_cycle, (labels, ranks, u_first, v_first, u_second, v_second))
    updated = updated.at[0, 0].set(first_sol).at[0, 1].set(second_sol)
    return (updated, jnp.stack([first_lower, second_lower]))
```

```python
import functools
import math

import jax
import jax.numpy as jnp
from jax import lax
from jax.experimental import pallas as pl
from jax.experimental.pallas import tpu as pltpu
from jax.sharding import PartitionSpec as P

NRHS = 256
NB = 128
RADIX = 8
F32 = jnp.float32
BF16 = jnp.bfloat16
four_pi = 4.0 * math.pi


def split(x):
    high = x.astype(BF16)
    return high, (x - high.astype(F32)).astype(BF16)


def dg(a, b, ca=1, cb=0):
    return lax.dot_general(a, b, (((ca,), (cb,)), ((), ())), preferred_element_type=F32)


def mm3(a, b, ca=1, cb=0):
    ah, al = split(a)
    bh, bl = split(b)
    return dg(ah, bh, ca, cb) + (dg(ah, bl, ca, cb) + dg(al, bh, ca, cb))


def mm_left(a, b, ca=1, cb=0):
    ah, al = split(a)
    return dg(ah, b, ca, cb) + dg(al, b, ca, cb)


def mm_right(a, b, ca=1, cb=0):
    bh, bl = split(b)
    return dg(a, bh, ca, cb) + dg(a, bl, ca, cb)


def columns_of(rows):
    pad = jnp.zeros((128 - rows.shape[0], rows.shape[1]), F32)
    return jnp.concatenate([rows, pad], axis=0).T


def kernel_tile(points):
    spots = points.astype(F32)
    n = spots.shape[1]
    cols = columns_of(spots)
    distance = jnp.zeros((n, n), F32)
    for dimension in range(3):
        offset = cols[:, dimension : dimension + 1] - spots[dimension : dimension + 1, :]
        distance = distance + offset * offset
    eye = eye_of(n)
    return lax.rsqrt(distance + 1.0) * (1.0 / four_pi) + eye


def eye_of(n):
    row = lax.broadcasted_iota(jnp.int32, (n, n), 0)
    col = lax.broadcasted_iota(jnp.int32, (n, n), 1)
    return jnp.where(row == col, 1.0, 0.0).astype(F32)


def onehot(label_column, dtype=F32):
    n = label_column.shape[0]
    lanes = lax.broadcasted_iota(jnp.int32, (n, NRHS), 1).astype(F32)
    return jnp.where(label_column == lanes, 1.0, 0.0).astype(dtype)


def sweep(blocks, out_refs):
    lane = lax.broadcasted_iota(jnp.int32, (1, NB), 1)
    active = list(blocks)
    for start in range(0, NB, RADIX):
        base = (start // 8) * 8
        off = start - base
        for which in range(len(active)):
            act = active[which]
            if off == 0 and start > 0:
                act = act[8:, :]
            cols = [
                jnp.broadcast_to(act[:, start + k : start + k + 1], act.shape) for k in range(RADIX)
            ]
            rows = [act[off + k : off + k + 1, :] for k in range(RADIX)]
            for k in range(RADIX):
                j = start + k
                pivot = cols[k][off + k : off + k + 1, :]
                root = lax.rsqrt(pivot)
                inverse = root * root
                scaled = jnp.where(lane == j, pivot + 1.0, rows[k]) * inverse
                final = jnp.where(lane < j, rows[k], jnp.where(lane == j, 1.0, 0.0)) * root
                out_refs[which][j : j + 1, :] = final
                for m in range(k + 1, RADIX):
                    entry = cols[k][off + m : off + m + 1, :]
                    rows[m] = rows[m] - entry * scaled
                    cols[m] = cols[m] - cols[k] * (entry * inverse)
                act = act - cols[k] * scaled
            active[which] = act


def factor(mats, inverses):
    height = mats[0].shape[0]
    steps = height // NB

    def step(b, carry):
        at = pl.ds(pl.multiple_of(b * NB, NB), NB)
        sweep([mat[at, at] for mat in mats], inverses)
        for s in range(steps):

            @pl.when(b == s)
            def _():
                lo, hi = s * NB, (s + 1) * NB
                for mat, inv in zip(mats, inverses):
                    panel = mm3(inv[...], mat[lo:hi, lo : height + hi])
                    mat[lo:hi, lo : height + hi] = panel
                    if hi < height:
                        left = panel[:, NB : height - lo]
                        mat[hi:, hi : height + hi] -= mm3(left, panel[:, NB:], 0, 0)

        return carry

    lax.fori_loop(0, steps, step, 0)


def triangle(upper):
    n = upper.shape[0]
    row = lax.broadcasted_iota(jnp.int32, (n, n), 0)
    col = lax.broadcasted_iota(jnp.int32, (n, n), 1)
    return jnp.where(row <= col, upper, 0.0)


def first_kernel(coords, mat, inverse):
    height = mat.shape[0]
    mat[:, :height] = kernel_tile(coords[0])
    mat[:, height:] = eye_of(height)
    factor([mat], [inverse])


def second_kernel(
    place, ranks, coords, labels, payload, first, u0, v0, u1, v1, out, diag,
    mat, inverse, lowers, heads, tails, lead, label_cols, sem,
):
    step = pl.program_id(0)
    height = mat.shape[0]
    rmax = u0.shape[-1]

    @pl.when(step == 0)
    def _():
        label_cols[...] = columns_of(labels[...].astype(F32))
        u_one = payload[:height, :rmax]
        v_one = payload[:height, rmax : 2 * rmax]
        marks = columns_of(payload[height : height + 16, :].astype(F32))
        b_zero = onehot(jnp.concatenate([marks[:, 0:1], marks[:, 1:2]], axis=0), BF16)
        b_one = onehot(jnp.concatenate([marks[:, 2:3], marks[:, 3:4]], axis=0))
        lower_inverse = first[:, height:]
        lowers[0] = triangle(first[:, :height]).T
        w_y = mm_left(lower_inverse, jnp.concatenate([v_one, b_zero], axis=1))
        gram = mm3(w_y[:, :rmax], w_y, 0, 0)
        spread = mm_right(u_one, gram)
        mat[:, :height] = kernel_tile(coords[1]) - mm_left(spread[:, :rmax], u_one, 1, 1)
        mat[:, height:] = eye_of(height)
        factor([mat], [inverse])
        second_inverse = mat[:, height:]
        y_one = mm3(second_inverse, b_one - spread[:, rmax:])
        lead[0] = w_y[:, rmax:]
        lead[1] = y_one
        lowers[1] = triangle(mat[:, :height]).T
        pltpu.make_async_copy(lowers, diag, sem).start()
        z_one = mm3(second_inverse, y_one, 0, 0)
        g_z = mm3(lower_inverse, w_y, 0, 0)
        blend = g_z[:, rmax:] - mm3(g_z[:, :rmax], mm_right(u_one, z_one, 0, 0))
        high, low = split(blend)
        heads[:, :NRHS] = high
        heads[:, NRHS:] = low
        high, low = split(z_one)
        tails[:, :NRHS] = high
        tails[:, NRHS:] = low

    lanes = lax.broadcasted_iota(jnp.int32, (height, rmax), 1)
    zero = jnp.zeros((), BF16)
    v_zero = jnp.where(lanes < ranks[step, 0], v0[0, 0], zero)
    v_next = jnp.where(lanes < ranks[step, 1], v1[0, 0], zero)
    m_zero = dg(v_zero, heads[...], 0, 0)
    m_next = dg(v_next, tails[...], 0, 0)
    weights = jnp.concatenate(
        [m_zero[:, :NRHS] + m_zero[:, NRHS:], m_next[:, :NRHS] + m_next[:, NRHS:]], axis=0
    )
    pair = jnp.concatenate([u0[0, 0], u1[0, 0]], axis=1)
    all_lanes = lax.broadcasted_iota(jnp.int32, label_cols.shape, 1)
    mark = jnp.sum(jnp.where(all_lanes == step, label_cols[...], 0.0), axis=1, keepdims=True)
    out[0, 0] = onehot(mark) - mm_right(pair, weights)

    @pl.when(jnp.logical_and(step == 0, place[0] < 2))
    def _():
        out[0, 0] = lead[place[0]]

    @pl.when(step == pl.num_programs(0) - 1)
    def _():
        pltpu.make_async_copy(lowers, diag, sem).wait()


def local(coords, labels, ranks, u_first, v_first, u_second, v_second):
    position = lax.axis_index("row")
    cycles, _, height, rmax = u_first.shape
    vmem = pltpu.CompilerParams(vmem_limit_bytes=56 * 1024 * 1024)
    zero = jnp.zeros((), BF16)
    keep = jnp.arange(rmax) < ranks[0, 0, 0]
    factors = jnp.concatenate(
        [u_first[0, 0], jnp.where(keep[None, :], v_first[0, 0], zero)], axis=1
    )
    mark = labels[0, 0].astype(BF16).reshape(height // NRHS, NRHS)
    mark_rows = jnp.concatenate(
        [
            jnp.where(position == 0, mark, zero),
            jnp.where(position == 1, mark, zero),
            jnp.zeros((16 - 2 * (height // NRHS), NRHS), BF16),
        ],
        axis=0,
    )
    payload = jnp.concatenate([jnp.where(position == 1, factors, zero), mark_rows], axis=0)
    payload = lax.psum(payload, "row")

    first = pl.pallas_call(
        first_kernel,
        out_shape=jax.ShapeDtypeStruct((height, 2 * height), F32),
        scratch_shapes=[pltpu.VMEM((NB, NB), F32)],
        compiler_params=vmem,
        cost_estimate=pl.CostEstimate(flops=40_000_000_000, bytes_accessed=2**21, transcendentals=0),
        name="first_factor",
    )(coords)

    tile = lambda width: pl.BlockSpec((1, 1, height, width), lambda i: (i, 0, 0, 0))
    whole = pl.BlockSpec(memory_space=pltpu.VMEM)
    smem = pl.BlockSpec(memory_space=pltpu.SMEM)
    updated, diag = pl.pallas_call(
        second_kernel,
        grid=(cycles,),
        out_shape=(
            jax.ShapeDtypeStruct((cycles, 1, height, NRHS), F32),
            jax.ShapeDtypeStruct((2, height, height), F32),
        ),
        in_specs=[smem, smem, whole, whole, whole, whole] + [tile(rmax)] * 4,
        out_specs=(tile(NRHS), pl.BlockSpec(memory_space=pl.ANY)),
        scratch_shapes=[
            pltpu.VMEM((height, 2 * height), F32),
            pltpu.VMEM((NB, NB), F32),
            pltpu.VMEM((2, height, height), F32),
            pltpu.VMEM((height, 2 * NRHS), BF16),
            pltpu.VMEM((height, 2 * NRHS), BF16),
            pltpu.VMEM((2, height, NRHS), F32),
            pltpu.VMEM((height, 128), F32),
            pltpu.SemaphoreType.DMA,
        ],
        compiler_params=vmem,
        name="second_factor_and_tiles",
    )(
        position.reshape(1).astype(jnp.int32),
        ranks[:, 0],
        coords,
        labels[:, 0],
        payload,
        first,
        u_first,
        v_first,
        u_second,
        v_second,
    )
    return updated, diag


def solution(mesh):
    in_specs = (
        P("parts", None, None),
        P("parts", "row", None),
        P("parts", "row", None),
        P("parts", "row", None, None),
        P("parts", "row", None, None),
        P("parts", "row", None, None),
        P("parts", "row", None, None),
    )
    out_specs = (P("parts", "row", None, None), P("parts", None, None))
    return jax.shard_map(local, mesh=mesh, in_specs=in_specs, out_specs=out_specs, check_vma=False)
```

```python
import math

import jax
import jax.numpy as jnp
from jax import lax
from jax.experimental import pallas as pl
from jax.experimental.pallas import tpu as pltpu
from jax.sharding import PartitionSpec as P

NRHS = 256
NB = 128
RADIX = 8
F32 = jnp.float32
BF16 = jnp.bfloat16
four_pi = 4.0 * math.pi


def split(x):
    high = x.astype(BF16)
    return high, (x - high.astype(F32)).astype(BF16)


def dg(a, b, ca=1, cb=0):
    return lax.dot_general(a, b, (((ca,), (cb,)), ((), ())), preferred_element_type=F32)


def mm3(a, b, ca=1, cb=0):
    ah, al = split(a)
    bh, bl = split(b)
    return dg(ah, bh, ca, cb) + (dg(ah, bl, ca, cb) + dg(al, bh, ca, cb))


def mm_left(a, b, ca=1, cb=0):
    ah, al = split(a)
    return dg(ah, b, ca, cb) + dg(al, b, ca, cb)


def mm_right(a, b, ca=1, cb=0):
    bh, bl = split(b)
    return dg(a, bh, ca, cb) + dg(a, bl, ca, cb)


def columns_of(rows):
    pad = jnp.zeros((128 - rows.shape[0], rows.shape[1]), F32)
    return jnp.concatenate([rows, pad], axis=0).T


def kernel_tile(points):
    spots = points.astype(F32)
    n = spots.shape[1]
    cols = columns_of(spots)
    distance = jnp.zeros((n, n), F32)
    for dimension in range(3):
        offset = cols[:, dimension : dimension + 1] - spots[dimension : dimension + 1, :]
        distance = distance + offset * offset
    eye = eye_of(n)
    return lax.rsqrt(distance + 1.0) * (1.0 / four_pi) + eye


def eye_of(n):
    row = lax.broadcasted_iota(jnp.int32, (n, n), 0)
    col = lax.broadcasted_iota(jnp.int32, (n, n), 1)
    return jnp.where(row == col, 1.0, 0.0).astype(F32)


def onehot(label_column, dtype=F32):
    n = label_column.shape[0]
    lanes = lax.broadcasted_iota(jnp.int32, (n, NRHS), 1).astype(F32)
    return jnp.where(label_column == lanes, 1.0, 0.0).astype(dtype)


def sweep(blocks, out_refs):
    lane = lax.broadcasted_iota(jnp.int32, (1, NB), 1)
    active = list(blocks)
    for start in range(0, NB, RADIX):
        base = (start // 8) * 8
        off = start - base
        for which in range(len(active)):
            act = active[which]
            if off == 0 and start > 0:
                act = act[8:, :]
            cols = [
                jnp.broadcast_to(act[:, start + k : start + k + 1], act.shape) for k in range(RADIX)
            ]
            rows = [act[off + k : off + k + 1, :] for k in range(RADIX)]
            for k in range(RADIX):
                j = start + k
                pivot = cols[k][off + k : off + k + 1, :]
                root = lax.rsqrt(pivot)
                inverse = root * root
                scaled = jnp.where(lane == j, pivot + 1.0, rows[k]) * inverse
                final = jnp.where(lane < j, rows[k], jnp.where(lane == j, 1.0, 0.0)) * root
                out_refs[which][j : j + 1, :] = final
                for m in range(k + 1, RADIX):
                    entry = cols[k][off + m : off + m + 1, :]
                    rows[m] = rows[m] - entry * scaled
                    cols[m] = cols[m] - cols[k] * (entry * inverse)
                act = act - cols[k] * scaled
            active[which] = act


def factor(mats, inverses, after_first=None):
    height = mats[0].shape[0]
    steps = height // NB

    def step(b, carry):
        at = pl.ds(pl.multiple_of(b * NB, NB), NB)
        sweep([mat[at, at] for mat in mats], inverses)
        for s in range(steps):

            @pl.when(b == s)
            def _():
                lo, hi = s * NB, (s + 1) * NB
                for mat, inv in zip(mats, inverses):
                    panel = mm3(inv[...], mat[lo:hi, lo : height + hi])
                    mat[lo:hi, lo : height + hi] = panel
                    if hi < height:
                        left = panel[:, NB : height - lo]
                        mat[hi:, hi : height + hi] -= mm3(left, panel[:, NB:], 0, 0)

        if after_first is not None:
            pl.when(b == 0)(after_first)
        return carry

    lax.fori_loop(0, steps, step, 0)


def triangle(upper):
    n = upper.shape[0]
    row = lax.broadcasted_iota(jnp.int32, (n, n), 0)
    col = lax.broadcasted_iota(jnp.int32, (n, n), 1)
    return jnp.where(row <= col, upper, 0.0)


def first_kernel(
    ranks, coords, labels, u_tile, v_tile, mat, pay_out, marks_out,
    inverse, pay, marks, scatter_send, scatter_recv, gather_send, gather_recv, mark_send, mark_recv,
):
    me = lax.axis_index("row")
    number = lax.axis_size("row")
    height = mat.shape[0]
    rmax = pay.shape[1]
    rows = pay.shape[0] // number
    mesh_id = pl.DeviceIdType.MESH

    def others(body):
        def at(d, carry):
            body(lax.rem(me + d, number))
            return carry

        lax.fori_loop(1, number, at, 0)

    def piece(owner):
        return pay.at[pl.ds(pl.multiple_of(owner * rows, rows), rows)]

    def scatter(to):
        return pltpu.make_async_remote_copy(
            src_ref=piece(to), dst_ref=piece(to), send_sem=scatter_send.at[to],
            recv_sem=scatter_recv, device_id={"row": to}, device_id_type=mesh_id,
        )

    def gather(owner, to):
        return pltpu.make_async_remote_copy(
            src_ref=piece(owner), dst_ref=piece(owner), send_sem=gather_send.at[to],
            recv_sem=gather_recv.at[owner], device_id={"row": to}, device_id_type=mesh_id,
        )

    def mark(slot, to):
        return pltpu.make_async_remote_copy(
            src_ref=marks.at[slot], dst_ref=marks.at[slot], send_sem=mark_send.at[to],
            recv_sem=mark_recv.at[slot], device_id={"row": to}, device_id_type=mesh_id,
        )

    barrier = pltpu.get_barrier_semaphore()
    others(
        lambda to: pl.semaphore_signal(
            barrier, inc=1, device_id={"row": to}, device_id_type=mesh_id
        )
    )
    for slot in range(2):

        @pl.when(me == slot)
        def _():
            marks[slot] = labels[0:1, :]

    @pl.when(me == 1)
    def _():
        lanes = lax.broadcasted_iota(jnp.int32, (height, rmax), 1)
        pay[:height, :] = u_tile[0, 0]
        pay[height:, :] = jnp.where(lanes < ranks[0, 0], v_tile[0, 0], jnp.zeros((), BF16))

    pl.semaphore_wait(barrier, number - 1)

    @pl.when(me == 1)
    def _():
        others(lambda to: scatter(to).start())

    for slot in range(2):

        @pl.when(me == slot)
        def _():
            others(lambda to: mark(slot, to).start())

    mat[:, :height] = kernel_tile(coords[0])
    mat[:, height:] = eye_of(height)

    def pass_on():
        @pl.when(me != 1)
        def _():
            scatter(me).wait_recv()

        def send(to):
            @pl.when(to != 1)
            def _():
                gather(me, to).start()

        others(send)

    factor([mat], [inverse], pass_on)

    @pl.when(me != 1)
    def _():
        others(lambda owner: gather(owner, me).wait_recv())

    @pl.when(me == 1)
    def _():
        others(lambda to: scatter(to).wait_send())

    for slot in range(2):

        @pl.when(me == slot)
        def _():
            others(lambda to: mark(slot, to).wait_send())

        @pl.when(me != slot)
        def _():
            mark(slot, me).wait_recv()

    def sent(to):
        @pl.when(to != 1)
        def _():
            gather(me, to).wait_send()

    others(sent)
    pay_out[...] = pay[...]
    marks_out[...] = marks[...]


def second_kernel(
    place, ranks, coords, labels, payload, marks, first, u0, v0, u1, v1, out, diag,
    mat, inverse, lowers, heads, tails, lead, label_cols, sem,
):
    step = pl.program_id(0)
    height = mat.shape[0]
    rmax = u0.shape[-1]

    @pl.when(step == 0)
    def _():
        label_cols[...] = columns_of(labels[...].astype(F32))
        u_one = payload[:height, :]
        v_one = payload[height:, :]
        marked = columns_of(jnp.concatenate([marks[0], marks[1]], axis=0).astype(F32))
        b_zero = onehot(marked[:, 0:1], BF16)
        b_one = onehot(marked[:, 1:2])
        lower_inverse = first[:, height:]
        lowers[0] = triangle(first[:, :height]).T
        w_y = mm_left(lower_inverse, jnp.concatenate([v_one, b_zero], axis=1))
        gram = mm3(w_y[:, :rmax], w_y, 0, 0)
        spread = mm_right(u_one, gram)
        mat[:, :height] = kernel_tile(coords[1]) - mm_left(spread[:, :rmax], u_one, 1, 1)
        mat[:, height:] = eye_of(height)
        factor([mat], [inverse])
        second_inverse = mat[:, height:]
        y_one = mm3(second_inverse, b_one - spread[:, rmax:])
        lead[0] = w_y[:, rmax:]
        lead[1] = y_one
        lowers[1] = triangle(mat[:, :height]).T
        pltpu.make_async_copy(lowers, diag, sem).start()
        z_one = mm3(second_inverse, y_one, 0, 0)
        g_z = mm3(lower_inverse, w_y, 0, 0)
        blend = g_z[:, rmax:] - mm3(g_z[:, :rmax], mm_right(u_one, z_one, 0, 0))
        high, low = split(blend)
        heads[:, :NRHS] = high
        heads[:, NRHS:] = low
        high, low = split(z_one)
        tails[:, :NRHS] = high
        tails[:, NRHS:] = low

    lanes = lax.broadcasted_iota(jnp.int32, (height, rmax), 1)
    zero = jnp.zeros((), BF16)
    v_zero = jnp.where(lanes < ranks[step, 0], v0[0, 0], zero)
    v_next = jnp.where(lanes < ranks[step, 1], v1[0, 0], zero)
    m_zero = dg(v_zero, heads[...], 0, 0)
    m_next = dg(v_next, tails[...], 0, 0)
    weights = jnp.concatenate(
        [m_zero[:, :NRHS] + m_zero[:, NRHS:], m_next[:, :NRHS] + m_next[:, NRHS:]], axis=0
    )
    pair = jnp.concatenate([u0[0, 0], u1[0, 0]], axis=1)
    all_lanes = lax.broadcasted_iota(jnp.int32, label_cols.shape, 1)
    mark = jnp.sum(jnp.where(all_lanes == step, label_cols[...], 0.0), axis=1, keepdims=True)
    out[0, 0] = onehot(mark) - mm_right(pair, weights)

    @pl.when(jnp.logical_and(step == 0, place[0] < 2))
    def _():
        out[0, 0] = lead[place[0]]

    @pl.when(step == pl.num_programs(0) - 1)
    def _():
        pltpu.make_async_copy(lowers, diag, sem).wait()


def local(coords, labels, ranks, u_first, v_first, u_second, v_second):
    position = lax.axis_index("row")
    cycles, _, height, rmax = u_first.shape
    vmem = pltpu.CompilerParams(vmem_limit_bytes=56 * 1024 * 1024)
    number = lax.axis_size("row")
    whole = pl.BlockSpec(memory_space=pltpu.VMEM)
    smem = pl.BlockSpec(memory_space=pltpu.SMEM)
    lead_tile = pl.BlockSpec((1, 1, height, rmax), lambda i: (0, 0, 0, 0))
    first, payload, marks = pl.pallas_call(
        first_kernel,
        grid=(1,),
        out_shape=(
            jax.ShapeDtypeStruct((height, 2 * height), F32),
            jax.ShapeDtypeStruct((2 * height, rmax), BF16),
            jax.ShapeDtypeStruct((2, 1, height), jnp.int32),
        ),
        in_specs=[smem, whole, whole, lead_tile, lead_tile],
        out_specs=(whole, whole, whole),
        scratch_shapes=[
            pltpu.VMEM((NB, NB), F32),
            pltpu.VMEM((2 * height, rmax), BF16),
            pltpu.VMEM((2, 1, height), jnp.int32),
            pltpu.SemaphoreType.DMA((number,)),
            pltpu.SemaphoreType.DMA,
            pltpu.SemaphoreType.DMA((number,)),
            pltpu.SemaphoreType.DMA((number,)),
            pltpu.SemaphoreType.DMA((number,)),
            pltpu.SemaphoreType.DMA((2,)),
        ],
        compiler_params=pltpu.CompilerParams(
            vmem_limit_bytes=48 * 1024 * 1024, collective_id=0, has_side_effects=True
        ),
        name="first_factor_and_spread",
    )(ranks[:, 0], coords, labels[:, 0], u_first, v_first)

    tile = lambda width: pl.BlockSpec((1, 1, height, width), lambda i: (i, 0, 0, 0))
    updated, diag = pl.pallas_call(
        second_kernel,
        grid=(cycles,),
        out_shape=(
            jax.ShapeDtypeStruct((cycles, 1, height, NRHS), F32),
            jax.ShapeDtypeStruct((2, height, height), F32),
        ),
        in_specs=[smem, smem, whole, whole, whole, whole, whole] + [tile(rmax)] * 4,
        out_specs=(tile(NRHS), pl.BlockSpec(memory_space=pl.ANY)),
        scratch_shapes=[
            pltpu.VMEM((height, 2 * height), F32),
            pltpu.VMEM((NB, NB), F32),
            pltpu.VMEM((2, height, height), F32),
            pltpu.VMEM((height, 2 * NRHS), BF16),
            pltpu.VMEM((height, 2 * NRHS), BF16),
            pltpu.VMEM((2, height, NRHS), F32),
            pltpu.VMEM((height, 128), F32),
            pltpu.SemaphoreType.DMA,
        ],
        compiler_params=vmem,
        name="second_factor_and_tiles",
    )(
        position.reshape(1).astype(jnp.int32),
        ranks[:, 0],
        coords,
        labels[:, 0],
        payload,
        marks,
        first,
        u_first,
        v_first,
        u_second,
        v_second,
    )
    return updated, diag


def solution(mesh):
    in_specs = (
        P("parts", None, None),
        P("parts", "row", None),
        P("parts", "row", None),
        P("parts", "row", None, None),
        P("parts", "row", None, None),
        P("parts", "row", None, None),
        P("parts", "row", None, None),
    )
    out_specs = (P("parts", "row", None, None), P("parts", None, None))
    return jax.shard_map(local, mesh=mesh, in_specs=in_specs, out_specs=out_specs, check_vma=False)
```

```python
import math

import jax
import jax.numpy as jnp
from jax import lax
from jax.experimental import pallas as pl
from jax.experimental.pallas import tpu as pltpu
from jax.sharding import PartitionSpec as P

NRHS = 256
NB = 128
RADIX = 4
VMEM_BYTES = 60 * 1024 * 1024
F32 = jnp.float32
BF16 = jnp.bfloat16
four_pi = 4.0 * math.pi


def split(x):
    high = x.astype(BF16)
    return high, (x - high.astype(F32)).astype(BF16)


def dg(a, b, ca=1, cb=0):
    return lax.dot_general(a, b, (((ca,), (cb,)), ((), ())), preferred_element_type=F32)


def mm3(a, b, ca=1, cb=0):
    ah, al = split(a)
    bh, bl = split(b)
    return dg(ah, bh, ca, cb) + (dg(ah, bl, ca, cb) + dg(al, bh, ca, cb))


def mm_left(a, b, ca=1, cb=0):
    ah, al = split(a)
    return dg(ah, b, ca, cb) + dg(al, b, ca, cb)


def mm_right(a, b, ca=1, cb=0):
    bh, bl = split(b)
    return dg(a, bh, ca, cb) + dg(a, bl, ca, cb)


def columns_of(rows):
    pad = jnp.zeros((128 - rows.shape[0], rows.shape[1]), F32)
    return jnp.concatenate([rows, pad], axis=0).T


def kernel_tile(points):
    spots = points.astype(F32)
    n = spots.shape[1]
    cols = columns_of(spots)
    distance = jnp.zeros((n, n), F32)
    for dimension in range(3):
        offset = cols[:, dimension : dimension + 1] - spots[dimension : dimension + 1, :]
        distance = distance + offset * offset
    eye = eye_of(n)
    return lax.rsqrt(distance + 1.0) * (1.0 / four_pi) + eye


def eye_of(n):
    row = lax.broadcasted_iota(jnp.int32, (n, n), 0)
    col = lax.broadcasted_iota(jnp.int32, (n, n), 1)
    return jnp.where(row == col, 1.0, 0.0).astype(F32)


def onehot(label_column, dtype=F32):
    n = label_column.shape[0]
    lanes = lax.broadcasted_iota(jnp.int32, (n, NRHS), 1).astype(F32)
    return jnp.where(label_column == lanes, 1.0, 0.0).astype(dtype)


def sweep(blocks, out_refs):
    lane = lax.broadcasted_iota(jnp.int32, (1, NB), 1)
    active = list(blocks)
    every = range(len(active))
    for start in range(0, NB, RADIX):
        off = start % 8
        if off == 0 and start > 0:
            active = [act[8:, :] for act in active]
        cols = [
            [jnp.broadcast_to(act[:, start + k : start + k + 1], act.shape) for k in range(RADIX)]
            for act in active
        ]
        rows = [[act[off + k : off + k + 1, :] for k in range(RADIX)] for act in active]
        for k in range(RADIX):
            j = start + k
            for w in every:
                pivot = cols[w][k][off + k : off + k + 1, :]
                root = lax.rsqrt(pivot)
                inverse = root * root
                scaled = jnp.where(lane == j, pivot + 1.0, rows[w][k]) * inverse
                final = jnp.where(lane < j, rows[w][k], jnp.where(lane == j, 1.0, 0.0)) * root
                out_refs[w][j : j + 1, :] = final
                for m in range(k + 1, RADIX):
                    entry = cols[w][k][off + m : off + m + 1, :]
                    rows[w][m] = rows[w][m] - entry * scaled
                    cols[w][m] = cols[w][m] - cols[w][k] * (entry * inverse)
                active[w] = active[w] - cols[w][k] * scaled


def factor(mats, inverses):
    height = mats[0].shape[0]
    steps = height // NB

    def step(b, carry):
        at = pl.ds(pl.multiple_of(b * NB, NB), NB)
        sweep([mat[at, at] for mat in mats], inverses)
        for s in range(steps):

            @pl.when(b == s)
            def _():
                lo, hi = s * NB, (s + 1) * NB
                for mat, inv in zip(mats, inverses):
                    panel = mm3(inv[...], mat[lo:hi, lo : height + hi])
                    mat[lo:hi, lo : height + hi] = panel
                    if hi < height:
                        left = panel[:, NB : height - lo]
                        mat[hi:, hi : height + hi] -= mm3(left, panel[:, NB:], 0, 0)

        return carry

    lax.fori_loop(0, steps, step, 0)


def near_inverse(tile):
    n = tile.shape[0]
    top = 1.0 + n / four_pi
    rho = (top - 1.0) / (top + 1.0)
    scale = 2.0 / (1.0 + top)
    gain = 2.0 / (2.0 - rho * rho)
    inverse = (gain * scale) * (2.0 * eye_of(n) - scale * tile)
    rho = rho * rho / (2.0 - rho * rho)
    narrow = tile.astype(BF16)
    while rho > 0.05:
        gain = 2.0 / (2.0 - rho * rho)
        flat = inverse.astype(BF16)
        product = dg(narrow, flat).astype(BF16)
        inverse = gain * (2.0 * inverse - dg(flat, product))
        rho = rho * rho / (2.0 - rho * rho)
    return inverse


def refined(tile, inverse, target):
    flat = inverse.astype(BF16)
    solved = dg(flat, target.astype(BF16))
    for _ in range(6):
        solved = solved + dg(flat, (target - mm3(tile, solved)).astype(BF16))
    return solved


def triangle(upper):
    n = upper.shape[0]
    row = lax.broadcasted_iota(jnp.int32, (n, n), 0)
    col = lax.broadcasted_iota(jnp.int32, (n, n), 1)
    return jnp.where(row <= col, upper, 0.0)


def first_kernel(
    ranks, coords, labels, u_tile, v_tile, heads, tails, lead, lowers,
    mat_zero, mat_one, part_zero, part_one, pay, marks, scatter_send, scatter_recv, gather_send, gather_recv, mark_send, mark_recv,
):
    me = lax.axis_index("row")
    number = lax.axis_size("row")
    height = mat_zero.shape[0]
    rmax = pay.shape[1]
    rows = pay.shape[0] // number
    mesh_id = pl.DeviceIdType.MESH

    def others(body):
        def at(d, carry):
            body(lax.rem(me + d, number))
            return carry

        lax.fori_loop(1, number, at, 0)

    def piece(owner):
        return pay.at[pl.ds(pl.multiple_of(owner * rows, rows), rows)]

    def scatter(to):
        return pltpu.make_async_remote_copy(
            src_ref=piece(to), dst_ref=piece(to), send_sem=scatter_send.at[to],
            recv_sem=scatter_recv, device_id={"row": to}, device_id_type=mesh_id,
        )

    def gather(owner, to):
        return pltpu.make_async_remote_copy(
            src_ref=piece(owner), dst_ref=piece(owner), send_sem=gather_send.at[to],
            recv_sem=gather_recv.at[owner], device_id={"row": to}, device_id_type=mesh_id,
        )

    def mark(slot, to):
        return pltpu.make_async_remote_copy(
            src_ref=marks.at[slot], dst_ref=marks.at[slot], send_sem=mark_send.at[to],
            recv_sem=mark_recv.at[slot], device_id={"row": to}, device_id_type=mesh_id,
        )

    barrier = pltpu.get_barrier_semaphore()
    others(
        lambda to: pl.semaphore_signal(
            barrier, inc=1, device_id={"row": to}, device_id_type=mesh_id
        )
    )
    for slot in range(2):

        @pl.when(me == slot)
        def _():
            marks[slot] = labels[0]

    @pl.when(me == 1)
    def _():
        lanes = lax.broadcasted_iota(jnp.int32, (height, rmax), 1)
        pay[:height, :] = u_tile[0, 0]
        pay[height:, :] = jnp.where(lanes < ranks[0, 0, 0], v_tile[0, 0], jnp.zeros((), BF16))

    pl.semaphore_wait(barrier, number - 1)

    @pl.when(me == 1)
    def _():
        others(lambda to: scatter(to).start())

    for slot in range(2):

        @pl.when(me == slot)
        def _():
            others(lambda to: mark(slot, to).start())

    tile_zero = kernel_tile(coords[0])
    mat_zero[:, :height] = tile_zero
    mat_zero[:, height:] = eye_of(height)
    inverse = near_inverse(tile_zero)

    @pl.when(me != 1)
    def _():
        scatter(me).wait_recv()

    def send(to):
        @pl.when(to != 1)
        def _():
            gather(me, to).start()

    others(send)
    mat_one[:, :height] = kernel_tile(coords[1])
    mat_one[:, height:] = eye_of(height)

    @pl.when(me != 1)
    def _():
        others(lambda owner: gather(owner, me).wait_recv())

    @pl.when(me == 1)
    def _():
        others(lambda to: scatter(to).wait_send())

    for slot in range(2):

        @pl.when(me == slot)
        def _():
            others(lambda to: mark(slot, to).wait_send())

        @pl.when(me != slot)
        def _():
            mark(slot, me).wait_recv()

    def sent(to):
        @pl.when(to != 1)
        def _():
            gather(me, to).wait_send()

    others(sent)
    u_one = pay[:height, :]
    v_one = pay[height:, :]
    marked = columns_of(jnp.concatenate([marks[0], marks[1]], axis=0).astype(F32))
    b_zero = onehot(marked[:, 0:1], BF16)
    b_one = onehot(marked[:, 1:2])
    solved = refined(tile_zero, inverse, v_one.astype(F32))
    both = jnp.concatenate([v_one, b_zero], axis=1)
    spread = mm_right(u_one, mm_left(solved, both, 0, 0))
    mat_one[:, :height] -= mm_left(spread[:, :rmax], u_one, 1, 1)
    factor([mat_zero, mat_one], [part_zero, part_one])
    y_zero = mm_left(mat_zero[:, height:], b_zero)
    y_one = mm3(mat_one[:, height:], b_one - spread[:, rmax:])
    lead[0] = y_zero
    lead[1] = y_one
    lowers[0] = triangle(mat_zero[:, :height]).T
    lowers[1] = triangle(mat_one[:, :height]).T
    z_one = mm3(mat_one[:, height:], y_one, 0, 0)
    z_zero = mm3(mat_zero[:, height:], y_zero, 0, 0)
    blend = z_zero - mm3(solved, mm_right(u_one, z_one, 0, 0))
    high, low = split(blend)
    heads[:, :NRHS] = high
    heads[:, NRHS:] = low
    high, low = split(z_one)
    tails[:, :NRHS] = high
    tails[:, NRHS:] = low


def second_kernel(
    place, ranks, labels, heads, tails, lead, lowers, u0, v0, u1, v1, out, diag, label_cols, sem
):
    step = pl.program_id(0)
    height, rmax = u0.shape[2:]

    @pl.when(step == 0)
    def _():
        pltpu.make_async_copy(lowers, diag, sem).start()
        rows = [labels[i] for i in range(labels.shape[0])]
        label_cols[...] = columns_of(jnp.concatenate(rows, axis=0).astype(F32))

    lanes = lax.broadcasted_iota(jnp.int32, (height, rmax), 1)
    zero = jnp.zeros((), BF16)
    v_zero = jnp.where(lanes < ranks[step, 0, 0], v0[0, 0], zero)
    v_next = jnp.where(lanes < ranks[step, 0, 1], v1[0, 0], zero)
    m_zero = dg(v_zero, heads[...], 0, 0)
    m_next = dg(v_next, tails[...], 0, 0)
    weights = jnp.concatenate(
        [m_zero[:, :NRHS] + m_zero[:, NRHS:], m_next[:, :NRHS] + m_next[:, NRHS:]], axis=0
    )
    pair = jnp.concatenate([u0[0, 0], u1[0, 0]], axis=1)
    all_lanes = lax.broadcasted_iota(jnp.int32, label_cols.shape, 1)
    mark = jnp.sum(jnp.where(all_lanes == step, label_cols[...], 0.0), axis=1, keepdims=True)
    out[0, 0] = onehot(mark) - mm_right(pair, weights)

    @pl.when(jnp.logical_and(step == 0, place[0] < 2))
    def _():
        out[0, 0] = lead[place[0]]

    @pl.when(step == pl.num_programs(0) - 1)
    def _():
        pltpu.make_async_copy(lowers, diag, sem).wait()


def local(coords, labels, ranks, u_first, v_first, u_second, v_second):
    position = lax.axis_index("row")
    cycles, _, height, rmax = u_first.shape
    number = lax.axis_size("row")
    whole = pl.BlockSpec(memory_space=pltpu.VMEM)
    smem = pl.BlockSpec(memory_space=pltpu.SMEM)
    lead_tile = pl.BlockSpec((1, 1, height, rmax), lambda i: (0, 0, 0, 0))
    square = jax.ShapeDtypeStruct((height, 2 * NRHS), BF16)
    lower_shape = jax.ShapeDtypeStruct((2, height, height), F32)
    heads, tails, lead, lowers = pl.pallas_call(
        first_kernel,
        grid=(1,),
        out_shape=(
            square, square, jax.ShapeDtypeStruct((2, height, NRHS), F32), lower_shape,
        ),
        in_specs=[smem, whole, whole, lead_tile, lead_tile],
        out_specs=(whole,) * 4,
        scratch_shapes=[
            pltpu.VMEM((height, 2 * height), F32),
            pltpu.VMEM((height, 2 * height), F32),
            pltpu.VMEM((NB, NB), F32),
            pltpu.VMEM((NB, NB), F32),
            pltpu.VMEM((2 * height, rmax), BF16),
            pltpu.VMEM((2, 1, height), jnp.int32),
            pltpu.SemaphoreType.DMA((number,)),
            pltpu.SemaphoreType.DMA,
            pltpu.SemaphoreType.DMA((number,)),
            pltpu.SemaphoreType.DMA((number,)),
            pltpu.SemaphoreType.DMA((number,)),
            pltpu.SemaphoreType.DMA((2,)),
        ],
        compiler_params=pltpu.CompilerParams(
            vmem_limit_bytes=VMEM_BYTES, collective_id=0, has_side_effects=True
        ),
        name="both_factors",
    )(ranks, coords, labels, u_first, v_first)

    tile = lambda width: pl.BlockSpec((1, 1, height, width), lambda i: (i, 0, 0, 0))
    return pl.pallas_call(
        second_kernel,
        grid=(cycles,),
        out_shape=(jax.ShapeDtypeStruct((cycles, 1, height, NRHS), F32), lower_shape),
        in_specs=[smem, smem, whole, whole, whole, whole, pl.BlockSpec(memory_space=pl.ANY)]
        + [tile(rmax)] * 4,
        out_specs=(tile(NRHS), pl.BlockSpec(memory_space=pl.ANY)),
        scratch_shapes=[pltpu.VMEM((height, 128), F32), pltpu.SemaphoreType.DMA],
        compiler_params=pltpu.CompilerParams(vmem_limit_bytes=VMEM_BYTES),
        name="tiles",
    )(
        position.reshape(1).astype(jnp.int32),
        ranks,
        labels,
        heads,
        tails,
        lead,
        lowers,
        u_first,
        v_first,
        u_second,
        v_second,
    )


def solution(mesh):
    in_specs = (
        P("parts", None, None),
        P("parts", "row", None),
        P("parts", "row", None),
        P("parts", "row", None, None),
        P("parts", "row", None, None),
        P("parts", "row", None, None),
        P("parts", "row", None, None),
    )
    out_specs = (P("parts", "row", None, None), P("parts", None, None))
    return jax.shard_map(local, mesh=mesh, in_specs=in_specs, out_specs=out_specs, check_vma=False)
```
